512 devices in a mesh: img: 16 (over x, y_hi, core), txt: 32 (over y_lo, z).
Axes of the slice: x: 4, y: 4 (y_hi: 2, y_lo: 2; y = y_hi * 2 + y_lo), z: 16, core: 2. Of those that a mesh axis runs over, the one named last changes fastest.
Arguments:
- image_rows: bfloat16 [262144, 1152], P(('img', 'txt')), may hold values from -6 to 6
- text_rows: bfloat16 [262144, 1152], P(('img', 'txt')), may hold values from -6 to 6
- image_ids: int32 [262144], P(('img', 'txt')), may hold values from 0 to 511
- text_ids: int32 [262144], P(('img', 'txt')), may hold values from 0 to 511
- log_scale: float32 [1], replicated, may hold values from 4 to 4.8
- logit_bias: float32 [1], replicated, may hold values from -12 to -6
Outputs:
- row_loss: float32 [262144], P(('img', 'txt'))
- image_grad: bfloat16 [262144, 1152], P(('img', 'txt'))
- text_grad: bfloat16 [262144, 1152], P(('img', 'txt'))
The draws below stay inside these ranges and needn't reach their ends.
All inputs are finite; a program needn't handle non-finite values.
Results may differ from the reference program's by a relative error of at most 0.0078.
Values may be sent and summed in bfloat16 or wider, within the bound.
A program may use at most 64 MiB of HBM per device.

```python
import jax
import jax.numpy as jnp
from jax import lax

D = 1152
ROWS = 512
STEPS = 2
TOTAL = 262144
N_IMG = 16
N_TXT = 32


def set_ends(result, own_key, smallest, largest):
    dims = result.shape
    index_at = [jax.random.randint(jax.random.fold_in(own_key, axis), (), 0, dims[axis]) for axis in range(len(dims))]
    result = result.at[tuple(index_at)].set(smallest)
    longest = dims.index(max(dims))
    index_at[longest] = (index_at[longest] + 1) % dims[longest]
    return result.at[tuple(index_at)].set(largest)


def shard_levels(stream_key, shape, split, smallest, high):
    factor_of = 1.0
    for position, blocks in split:
        draws = jax.random.uniform(jax.random.fold_in(jax.random.fold_in(stream_key, 6), position), (blocks,), jnp.float32, smallest / len(split), high / len(split))
        factor_of = factor_of * jnp.repeat(jnp.exp(draws), shape[position] // blocks).reshape((-1,) + (1,) * (len(shape) - 1 - position))
    return factor_of


def noise(key, extent, width, limit, cuts=(), kind=jnp.bfloat16):
    array = jax.random.normal(key, extent, jnp.float32) * width
    if len(cuts) > 0:
        array = shard_levels(key, extent, cuts, -0.22, 0.18) * array
    return jnp.clip(array, min=-limit, max=limit).astype(kind)


def setup_inputs(seed: int = 0) -> dict:
    streams_of = jax.random.split(jax.random.key(seed), 7)
    image_rows = noise(streams_of[0], (TOTAL, D), 1.0, 6.0, ((0, 512),))
    text_rows = noise(streams_of[1], (TOTAL, D), 1.0, 6.0, ((0, 512),))
    image_ids = set_ends(jax.random.randint(streams_of[2], (TOTAL,), 0, ROWS), jax.random.fold_in(streams_of[2], 1), 0, ROWS - 1).astype(jnp.int32)
    text_ids = set_ends(jax.random.randint(streams_of[3], (TOTAL,), 0, ROWS), jax.random.fold_in(streams_of[3], 1), 0, ROWS - 1).astype(jnp.int32)
    log_scale = jnp.clip(jax.random.uniform(streams_of[4], (1,), jnp.float32, 4.0, 4.8), 4.0, 4.8)
    logit_bias = jnp.clip(jax.random.uniform(streams_of[5], (1,), jnp.float32, -12.0, -6.0), -12.0, -6.0)
    return {"image_rows": image_rows, "text_rows": text_rows, "image_ids": image_ids, "text_ids": text_ids, "log_scale": log_scale, "logit_bias": logit_bias}


def unit_rows(block_rows):
    widened = block_rows.astype(jnp.float32)
    inverse = lax.rsqrt(lax.optimization_barrier(jnp.sum(widened * widened, axis=1, keepdims=True)) + 1e-06)
    return ((widened * inverse).astype(jnp.bfloat16), inverse)

def pair_terms(image_unit, text_unit, image_tags, text_tags, logit_scale, bias_value):
    logits = logit_scale * jnp.dot(image_unit, text_unit.T, preferred_element_type=jnp.float32) + bias_value
    pair_signs = jnp.where(image_tags[:, None] == text_tags[None, :], 1.0, -1.0).astype(jnp.float32)
    margins = pair_signs * logits
    losses = lax.optimization_barrier(jnp.sum(jax.nn.softplus(-margins), axis=1))
    slopes = (-logit_scale * pair_signs * jax.nn.sigmoid(-margins)).astype(jnp.bfloat16)
    return (losses, slopes)

def back_norm(block_rows, inverse, unit_grad):
    widened = block_rows.astype(jnp.float32)
    inner_sum = lax.optimization_barrier(jnp.sum(widened * unit_grad, axis=1, keepdims=True))
    return (inverse * unit_grad - inverse * inverse * inverse * widened * inner_sum).astype(jnp.bfloat16)

def reference(image_rows, text_rows, image_ids, text_ids, log_scale, logit_bias):
    logit_scale = jnp.exp(log_scale[0])
    bias_value = logit_bias[0]
    image_blocks = image_rows.reshape(N_IMG, N_TXT, ROWS, D)
    text_blocks = text_rows.reshape(N_IMG, N_TXT, ROWS, D)
    image_tags = image_ids.reshape(N_IMG, N_TXT, ROWS)
    text_tags = text_ids.reshape(N_IMG, N_TXT, ROWS)

    def image_side(block_index):
        row_block = block_index // N_TXT
        col_block = block_index % N_TXT
        own_rows = image_blocks[row_block, col_block]
        own_unit, inverse = unit_rows(own_rows)
        loss_sum = jnp.zeros((ROWS,), jnp.float32)
        grad_sum = jnp.zeros((ROWS, D), jnp.float32)
        for step in range(STEPS):
            other_row = (row_block - step) % N_IMG
            other_col = (col_block + step) % N_TXT
            partner_unit, unused = unit_rows(text_blocks[other_row, other_col])
            losses, slopes = pair_terms(own_unit, partner_unit, image_tags[row_block, col_block], text_tags[other_row, other_col], logit_scale, bias_value)
            loss_sum = loss_sum + losses
            grad_sum = grad_sum + jnp.dot(slopes, partner_unit, preferred_element_type=jnp.float32)
        return (loss_sum, back_norm(own_rows, inverse, grad_sum))

    def text_side(block_index):
        row_block = block_index // N_TXT
        col_block = block_index % N_TXT
        own_rows = text_blocks[row_block, col_block]
        own_unit, inverse = unit_rows(own_rows)
        grad_sum = jnp.zeros((ROWS, D), jnp.float32)
        for step in range(STEPS):
            other_row = (row_block + step) % N_IMG
            other_col = (col_block - step) % N_TXT
            partner_unit, unused = unit_rows(image_blocks[other_row, other_col])
            losses, slopes = pair_terms(partner_unit, own_unit, image_tags[other_row, other_col], text_tags[row_block, col_block], logit_scale, bias_value)
            grad_sum = grad_sum + jnp.dot(slopes.T, partner_unit, preferred_element_type=jnp.float32)
        return back_norm(own_rows, inverse, grad_sum)
    block_range = jnp.arange(N_IMG * N_TXT, dtype=jnp.int32)
    row_loss, image_grad = lax.map(image_side, block_range)
    text_grad = lax.map(text_side, block_range)
    return (row_loss.reshape(N_IMG * N_TXT * ROWS), image_grad.reshape(N_IMG * N_TXT * ROWS, D), text_grad.reshape(N_IMG * N_TXT * ROWS, D))
```

```python
import functools

import jax
import jax.numpy as jnp
from jax import lax
from jax.experimental import pallas as pl
from jax.experimental.pallas import tpu as pltpu
from jax.sharding import PartitionSpec as P

MESH = pl.DeviceIdType.MESH
ROWS, D = 512, 1152
C = 128
CHUNKS = ROWS // C
NEAR, FAR = 0, 1


def inverse_norm(x):
    return lax.rsqrt(jnp.sum(x * x, axis=1, keepdims=True) + 1e-06)


def kernel(
    img, txt, img_ids, txt_ids, log_scale, logit_bias,
    loss_out, img_out, txt_out,
    own, unit, inv, got, acc, own_ids, got_ids, id_col, id_row, loss_acc,
    own_sem, own_id_sem, send_sem, recv_sem, id_send_sem, id_recv_sem,
):
    n_img, n_txt = lax.axis_size("img"), lax.axis_size("txt")
    p, q = lax.axis_index("img"), lax.axis_index("txt")
    core = lax.rem(p, 2)
    text_to = (lax.rem(p + 1, n_img), lax.rem(q + n_txt - 1, n_txt))
    image_to = (lax.rem(p + n_img - 1, n_img), lax.rem(q + 1, n_txt))

    barrier = pltpu.get_barrier_semaphore()
    for partner in (text_to, image_to):
        pl.semaphore_signal(barrier, inc=1, device_id=partner, device_id_type=MESH)

    def local_loads(sides):
        copies = []
        for side, (rows, ids) in enumerate(sides):
            copies.append(pltpu.make_async_copy(ids, own_ids.at[side], own_id_sem.at[side]))
            copies.append(pltpu.make_async_copy(rows, own.at[side], own_sem.at[side]))
        return copies

    def sends(sides, targets):
        copies = []
        for side, (rows, ids) in enumerate(sides):
            copies.append(
                pltpu.make_async_remote_copy(
                    src_ref=ids, dst_ref=got_ids.at[side],
                    send_sem=id_send_sem.at[side], recv_sem=id_recv_sem.at[side],
                    device_id=targets[side], device_id_type=MESH,
                )
            )
        for k in range(CHUNKS):
            for side, (rows, ids) in enumerate(sides):
                piece = pl.ds(k * C, C)
                copies.append(
                    pltpu.make_async_remote_copy(
                        src_ref=rows.at[piece], dst_ref=got.at[side, piece],
                        send_sem=send_sem.at[side, k], recv_sem=recv_sem.at[side, k],
                        device_id=targets[side], device_id_type=MESH,
                    )
                )
        return copies

    by_core = (
        (((txt, txt_ids), (img, img_ids)), (text_to, image_to)),
        (((img, img_ids), (txt, txt_ids)), (image_to, text_to)),
    )
    for c, (sides, targets) in enumerate(by_core):

        @pl.when(core == c)
        def _():
            for copy in local_loads(sides):
                copy.start()

    with jax.named_scope("barrier_wait"):
        pl.semaphore_wait(barrier, 2)

    for c, (sides, targets) in enumerate(by_core):

        @pl.when(core == c)
        def _():
            for copy in sends(sides, targets):
                copy.start()

    scale = jnp.exp(jnp.full((1, C), log_scale[0], jnp.float32))
    bias = logit_bias[0]

    for c, (sides, targets) in enumerate(by_core):

        @pl.when(core == c)
        def _():
            for copy in local_loads(sides):
                copy.wait()

    for side in (NEAR, FAR):
        for k in range(CHUNKS):
            piece = pl.ds(k * C, C)
            row = own_ids[side, piece].reshape(1, C)
            id_row[side, k] = jnp.broadcast_to(row, (8, C))
            id_col[side, piece, :] = jnp.broadcast_to(row, (C, C)).T

        @pl.loop(0, CHUNKS)
        def _(k):
            piece = pl.ds(k * C, C)
            x = own[side, piece, :].astype(jnp.float32)
            r = inverse_norm(x)
            inv[side, piece, :] = r
            unit[side, piece, :] = (x * r).astype(jnp.bfloat16)

    loss_acc[...] = jnp.zeros_like(loss_acc)
    acc[...] = jnp.zeros_like(acc)

    def slopes_of(side, other_unit, other_id_row, has_loss):
        logits = (
            lax.dot_general(
                unit[side], other_unit, (((1,), (1,)), ((), ())), preferred_element_type=jnp.float32
            )
            * scale
            + bias
        )
        same = id_col[side] == other_id_row
        margins = jnp.where(same, logits, -logits)
        e = jnp.exp(-jnp.abs(margins))
        recip = 1.0 / (1.0 + e)
        sigmoid = jnp.where(margins >= 0, e * recip, recip)

        @pl.when(has_loss)
        def _():
            loss_acc[...] += jnp.maximum(-margins, 0.0) + jnp.log1p(e)

        return (jnp.where(same, -scale, scale) * sigmoid).astype(jnp.bfloat16)

    def add_product(side, slopes, other_unit):
        acc[side] += jnp.dot(slopes, other_unit, preferred_element_type=jnp.float32)

    def has_loss(side):
        return core == (1 if side == NEAR else 0)

    for side in (NEAR, FAR):

        @pl.loop(0, CHUNKS)
        @jax.named_scope("own_pair_chunk")
        def _(k):
            other = unit[1 - side, pl.ds(k * C, C), :]
            slopes = slopes_of(side, other, id_row[1 - side, k][0:1], has_loss(side))
            add_product(side, slopes, other)

    for side in (NEAR, FAR):
        pltpu.make_async_remote_copy(
            src_ref=own_ids.at[side], dst_ref=got_ids.at[side],
            send_sem=id_send_sem.at[side], recv_sem=id_recv_sem.at[side],
            device_id=text_to, device_id_type=MESH,
        ).wait_recv()
        for k in range(CHUNKS):
            row = got_ids[side, pl.ds(k * C, C)].reshape(1, C)
            id_row[side, k] = jnp.broadcast_to(row, (8, C))

    def arrived(side, k):
        piece = pl.ds(k * C, C)
        pltpu.make_async_remote_copy(
            src_ref=own.at[side, piece], dst_ref=got.at[side, piece],
            send_sem=send_sem.at[side, k], recv_sem=recv_sem.at[side, k],
            device_id=text_to, device_id_type=MESH,
        ).wait_recv()
        x = got[side, piece, :].astype(jnp.float32)
        return (x * inverse_norm(x)).astype(jnp.bfloat16)

    @pl.loop(0, CHUNKS - 1)
    def _(k):
        for side, name in ((NEAR, "near"), (FAR, "far")):
            with jax.named_scope(f"{name}_chunk_wait"):
                other = arrived(side, k)
            with jax.named_scope(f"{name}_chunk"):
                slopes = slopes_of(side, other, id_row[side, k][0:1], has_loss(side))
                add_product(side, slopes, other)

    def finish(side, slopes, other, out):
        step = 128
        for b in range(ROWS // step):
            rows = pl.ds(b * step, step)
            g = acc[side, rows, :] + jnp.dot(
                slopes[b * step : (b + 1) * step], other, preferred_element_type=jnp.float32
            )
            x = own[side, rows, :].astype(jnp.float32)
            r = inv[side, rows, :]
            inner = jnp.sum(x * g, axis=1, keepdims=True)
            out[rows, :] = (r * g - (r * r * r * inner) * x).astype(jnp.bfloat16)

    for side, name in ((NEAR, "near"), (FAR, "far")):
        with jax.named_scope(f"last_{name}_chunk_wait"):
            other = arrived(side, CHUNKS - 1)
        with jax.named_scope(f"finish_{name}_side"):
            slopes = slopes_of(side, other, id_row[side, CHUNKS - 1][0:1], has_loss(side))
            for c, outs in enumerate(((txt_out, img_out), (img_out, txt_out))):
                pl.when(core == c)(functools.partial(finish, side, slopes, other, outs[side]))

    with jax.named_scope("loss_and_send_waits"):
        loss_out[...] = jnp.sum(loss_acc[...].T, axis=0, keepdims=True).reshape(ROWS)
        for c, (sides, targets) in enumerate(by_core):

            @pl.when(core == c)
            def _():
                for copy in sends(sides, targets):
                    copy.wait_send()


def body(image_rows, text_rows, image_ids, text_ids, log_scale, logit_bias):
    bf16, f32, i32 = jnp.bfloat16, jnp.float32, jnp.int32
    hbm = pl.BlockSpec(memory_space=pltpu.HBM)
    vmem = pl.BlockSpec(memory_space=pltpu.VMEM)
    operands = [
        pltpu.with_memory_space_constraint(x, pltpu.HBM)
        for x in (image_rows, text_rows, image_ids, text_ids)
    ]
    dma = pltpu.SemaphoreType.DMA
    return pl.pallas_call(
        kernel,
        out_shape=(
            pltpu.VMEM((ROWS,), f32),
            pltpu.VMEM((ROWS, D), bf16),
            pltpu.VMEM((ROWS, D), bf16),
        ),
        in_specs=[hbm] * 4 + [pl.BlockSpec(memory_space=pltpu.SMEM)] * 2,
        out_specs=(vmem,) * 3,
        scratch_shapes=[
            pltpu.VMEM((2, ROWS, D), bf16),
            pltpu.VMEM((2, ROWS, D), bf16),
            pltpu.VMEM((2, ROWS, 1), f32),
            pltpu.VMEM((2, ROWS, D), bf16),
            pltpu.VMEM((2, ROWS, D), f32),
            pltpu.VMEM((2, ROWS), i32),
            pltpu.VMEM((2, ROWS), i32),
            pltpu.VMEM((2, ROWS, C), i32),
            pltpu.VMEM((2, CHUNKS, 8, C), i32),
            pltpu.VMEM((ROWS, C), f32),
            dma((2,)), dma((2,)), dma((2, CHUNKS)), dma((2, CHUNKS)), dma((2,)), dma((2,)),
        ],
        compiler_params=pltpu.CompilerParams(
            collective_id=0, has_side_effects=True, vmem_limit_bytes=40 << 20
        ),
        name="exchange_and_grads",
    )(*operands, log_scale, logit_bias)


def solution(mesh):
    blocks = P(("img", "txt"))
    rows = P(("img", "txt"), None)
    return jax.shard_map(
        body,
        mesh=mesh,
        in_specs=(rows, rows, blocks, blocks, P(), P()),
        out_specs=(blocks, rows, rows),
        check_vma=False,
    )
```

```python
import jax
import jax.numpy as jnp
from jax import lax
from jax.experimental import pallas as pl
from jax.experimental.pallas import tpu as pltpu
from jax.sharding import PartitionSpec as P

MESH = pl.DeviceIdType.MESH
ROWS, D = 512, 1152
C = 128
FULL = ROWS // C - 1
HALF = C // 2
BLOCK = 128
TEXT, IMAGE = 0, 1


def inverse_norm(x):
    return lax.rsqrt(jnp.sum(x * x, axis=1, keepdims=True) + 1e-06)


def unit_rows(rows):
    x = rows.astype(jnp.float32)
    return (x * inverse_norm(x)).astype(jnp.bfloat16)


def slopes_of(own_unit, other_unit, same, scale, bias):
    dots = lax.dot_general(
        own_unit, other_unit, (((1,), (1,)), ((), ())), preferred_element_type=jnp.float32
    )
    logits = dots * scale + bias
    margins = jnp.where(same, logits, -logits)
    e = jnp.exp(-jnp.abs(margins))
    recip = 1.0 / (1.0 + e)
    sigmoid = jnp.where(margins >= 0, e * recip, recip)
    slopes = (jnp.where(same, -scale, scale) * sigmoid).astype(jnp.bfloat16)
    return slopes, dots, lambda: jnp.maximum(-margins, 0.0) + jnp.log1p(e)


def back_norm(rows, r, g):
    x = rows.astype(jnp.float32)
    inner = jnp.sum(x * g, axis=1, keepdims=True)
    return r * g - (r * r * r * inner) * x


def exchange_kernel(
    img, txt, img_ids, txt_ids, log_scale, logit_bias,
    loss, image_grad, text_own, text_unit, text_inv, text_base, last_unit, text_id_col, last_id_row, constants,
    image_own, image_unit, image_inv, image_acc, got, own_ids, got_ids, image_id_col, id_row, loss_acc,
    own_sem, own_id_sem, send_sem, recv_sem, id_send_sem, id_recv_sem, ack_sem,
):
    n_img, n_txt = lax.axis_size("img"), lax.axis_size("txt")
    p, q = lax.axis_index("img"), lax.axis_index("txt")
    text_to = (lax.rem(p + 1, n_img), lax.rem(q + n_txt - 1, n_txt))
    image_to = (lax.rem(p + n_img - 1, n_img), lax.rem(q + 1, n_txt))

    n_z = n_txt // 2
    z, core, y_hi = lax.rem(q, n_z), lax.rem(p, 2), lax.rem(p // 2, 2)
    near_to = (jnp.where(core == 0, text_to[0], image_to[0]), jnp.where(core == 0, text_to[1], image_to[1]))
    far_to = (jnp.where(core == 0, image_to[0], text_to[0]), jnp.where(core == 0, image_to[1], text_to[1]))
    first, last = jnp.int32(z == 0), jnp.int32(z == n_z - 1)
    both = jnp.where(core == 0, y_hi, 1 - y_hi)
    from_last = jnp.maximum(first, last)
    to_last = jnp.maximum(jnp.int32(z == n_z - 2), last)
    near_signals = jnp.where(core == 0, from_last, 1 - to_last)
    near_direct = 1 - near_signals
    near_acks = near_direct
    far_signals = jnp.where(core == 0, 1 - to_last, jnp.maximum(from_last, both))
    far_direct = jnp.where(core == 0, jnp.maximum(to_last, both), 1 - from_last)
    far_acks = jnp.where(core == 0, to_last, (1 - from_last) * (1 - both))
    image_direct = jnp.where(core == 0, far_direct, near_direct)
    text_direct = jnp.where(core == 0, near_direct, far_direct)

    barrier = pltpu.get_barrier_semaphore()
    for signals, partner in ((near_signals, near_to), (far_signals, far_to)):

        @pl.when(signals == 1)
        def _():
            pl.semaphore_signal(barrier, inc=1, device_id=partner, device_id_type=MESH)

    sources, source_ids, targets = (txt, img), (txt_ids, img_ids), (text_to, image_to)
    own, unit, inv, acc = (
        (image_own, text_own), (image_unit, text_unit), (image_inv, text_inv), (image_acc, text_base),
    )
    id_col = (image_id_col, text_id_col)
    pieces = (
        [(k * C, C) for k in range(FULL + 1)],
        [(k * C, C) for k in range(FULL)] + [(FULL * C, HALF), (FULL * C + HALF, HALF)],
    )

    def id_copy(side):
        return pltpu.make_async_remote_copy(
            src_ref=source_ids[side], dst_ref=got_ids.at[side],
            send_sem=id_send_sem.at[side], recv_sem=id_recv_sem.at[side],
            device_id=targets[side], device_id_type=MESH,
        )

    def piece_copy(side, k, start, size):
        rows = pl.ds(start, size)
        return pltpu.make_async_remote_copy(
            src_ref=sources[side].at[rows], dst_ref=got.at[side, rows],
            send_sem=send_sem.at[side, k], recv_sem=recv_sem.at[side, k],
            device_id=targets[side], device_id_type=MESH,
        )

    def sends(side):
        return [id_copy(side)] + [piece_copy(side, k, *piece) for k, piece in enumerate(pieces[side])]

    loads = []
    for side, ref, ids in ((TEXT, img, img_ids), (IMAGE, txt, txt_ids)):
        loads.append(pltpu.make_async_copy(ids, own_ids.at[side], own_id_sem.at[side]))
        loads.append(pltpu.make_async_copy(ref, own[side], own_sem.at[side]))
    for copy in loads:
        copy.start()

    def start_sends(side):
        for copy in sends(side):
            copy.start()

    n_direct = near_direct + far_direct

    @pl.when(n_direct > 0)
    def _():
        pl.semaphore_wait(barrier, n_direct)

    for i, (acks, partner) in enumerate(((near_acks, near_to), (far_acks, far_to))):

        @pl.when(acks == 1)
        def _():
            pl.semaphore_signal(ack_sem.at[i], inc=1, device_id=partner, device_id_type=MESH)

    image_ack = jnp.where(core == 0, 1, 0)
    pl.when(image_direct == 1)(lambda: start_sends(IMAGE))
    pl.when(text_direct == 1)(lambda: start_sends(TEXT))
    for side, direct, ack in ((IMAGE, image_direct, image_ack), (TEXT, text_direct, 1 - image_ack)):

        @pl.when(direct == 0)
        def _():
            pl.semaphore_wait(ack_sem.at[ack], 1)
            start_sends(side)

    scale = jnp.exp(jnp.full((1, C), log_scale[0], jnp.float32))
    bias = jnp.full((1, C), logit_bias[0], jnp.float32)
    constants[0:1, :] = scale
    constants[1:2, :] = bias

    for copy in loads:
        copy.wait()

    for side in (TEXT, IMAGE):
        for k in range(FULL + 1):
            piece = pl.ds(k * C, C)
            row = own_ids[side, piece].reshape(1, C)
            id_row[1 - side, k] = jnp.broadcast_to(row, (8, C))
            id_col[side][piece, :] = jnp.broadcast_to(row, (C, C)).T

        @pl.loop(0, FULL + 1)
        def _(k):
            piece = pl.ds(k * C, C)
            x = own[side][piece, :].astype(jnp.float32)
            r = inverse_norm(x)
            inv[side][piece, :] = jnp.broadcast_to(r, (C, C))
            unit[side][piece, :] = (x * r).astype(jnp.bfloat16)

    loss_acc[...] = jnp.zeros_like(loss_acc)
    for side in (TEXT, IMAGE):
        acc[side][...] = jnp.zeros_like(acc[side])

    def slopes_on(side, other_unit, other_ids):
        width = other_unit.shape[0]
        same = id_col[side][:, :width] == other_ids
        slopes, _, loss_terms = slopes_of(unit[side][...], other_unit, same, scale[:, :width], bias[:, :width])
        if side == TEXT:
            loss_acc[...] += loss_terms()
        return slopes

    def add_chunk(side, other_unit, other_ids):
        slopes = slopes_on(side, other_unit, other_ids)
        acc[side][...] += jnp.dot(slopes, other_unit, preferred_element_type=jnp.float32)

    for side in (TEXT, IMAGE):

        @pl.loop(0, FULL + 1)
        def _(k):
            add_chunk(side, unit[1 - side][pl.ds(k * C, C), :], id_row[side, k][0:1])

    for side in (TEXT, IMAGE):
        id_copy(side).wait_recv()
        for k in range(FULL + 1):
            row = got_ids[side, pl.ds(k * C, C)].reshape(1, C)
            id_row[side, k] = jnp.broadcast_to(row, (8, C))

    def arrived(side, k, start, size):
        piece_copy(side, k, start, size).wait_recv()
        return unit_rows(got[side, pl.ds(start, size), :])

    @pl.loop(0, FULL)
    def _(k):
        for side in (TEXT, IMAGE):
            other = arrived(side, k, k * C, C)
            add_chunk(side, other, id_row[side, k][0:1])

    def finish_text():
        other = arrived(TEXT, FULL, FULL * C, C)
        slopes = slopes_on(TEXT, other, id_row[TEXT, FULL][0:1])
        for b in range(ROWS // BLOCK):
            rows = pl.ds(b * BLOCK, BLOCK)
            g = image_acc[rows, :] + jnp.dot(
                slopes[b * BLOCK : (b + 1) * BLOCK], other, preferred_element_type=jnp.float32
            )
            grad = back_norm(image_own[rows, :], image_inv[rows, 0:1], g)
            image_grad[rows, :] = grad.astype(jnp.bfloat16)
        loss[...] = jnp.sum(loss_acc[...].T, axis=0, keepdims=True).reshape(ROWS)

    pl.when(first == 1)(finish_text)

    other = arrived(IMAGE, FULL, FULL * C, HALF)
    last_ids = id_row[IMAGE, FULL]
    add_chunk(IMAGE, other, last_ids[0:1, :HALF])
    last_id_row[...] = jnp.broadcast_to(last_ids[0:1, HALF:], (8, HALF))
    for b in range(ROWS // BLOCK):
        rows = pl.ds(b * BLOCK, BLOCK)
        text_base[rows, :] = back_norm(text_own[rows, :], text_inv[rows, 0:1], text_base[rows, :])

    pl.when(first == 0)(finish_text)

    for side in (TEXT, IMAGE):
        for copy in sends(side):
            copy.wait_send()
    last_unit[...] = arrived(IMAGE, FULL + 1, FULL * C + HALF, HALF)


def finish_kernel(
    loss, image_grad, own, unit, inv, base, last_unit, id_col, last_id_row, constants,
    loss_out, image_out, text_out,
    stage, sem,
):
    copies = [
        pltpu.make_async_copy(loss, loss_out, sem.at[0]),
        pltpu.make_async_copy(image_grad, image_out, sem.at[1]),
    ]
    for copy in copies:
        copy.start()
    other = last_unit[...]
    scale, bias = constants[0:1, :HALF], constants[1:2, :HALF]

    def slopes_and_inner(b):
        rows = pl.ds(b * BLOCK, BLOCK)
        same = id_col[rows, :HALF] == last_id_row[0:1]
        slopes, dots, _ = slopes_of(unit[rows, :], other, same, scale, bias)
        return slopes, jnp.sum(slopes.astype(jnp.float32) * dots, axis=1, keepdims=True)

    blocks = ROWS // BLOCK
    ahead = slopes_and_inner(0)
    for b in range(blocks):
        slopes, inner = ahead
        if b + 1 < blocks:
            ahead = slopes_and_inner(b + 1)
        rows = pl.ds(b * BLOCK, BLOCK)
        r = inv[rows, 0:1]
        h = jnp.dot(slopes, other, preferred_element_type=jnp.float32)
        grad = base[rows, :] + r * h - (r * r * inner) * own[rows, :].astype(jnp.float32)
        stage[rows, :] = grad.astype(jnp.bfloat16)
        copy = pltpu.make_async_copy(stage.at[rows], text_out.at[rows], sem.at[2 + b])
        copy.start()
        copies.append(copy)
    for copy in copies:
        copy.wait()


def body(image_rows, text_rows, image_ids, text_ids, log_scale, logit_bias):
    bf16, f32, i32 = jnp.bfloat16, jnp.float32, jnp.int32
    hbm = pl.BlockSpec(memory_space=pltpu.HBM)
    vmem = pl.BlockSpec(memory_space=pltpu.VMEM)
    smem = pl.BlockSpec(memory_space=pltpu.SMEM)
    dma = pltpu.SemaphoreType.DMA
    operands = [
        pltpu.with_memory_space_constraint(x, pltpu.HBM)
        for x in (image_rows, text_rows, image_ids, text_ids)
    ]
    handed_on = (
        pltpu.VMEM((ROWS,), f32),
        pltpu.VMEM((ROWS, D), bf16),
        pltpu.VMEM((ROWS, D), bf16),
        pltpu.VMEM((ROWS, D), bf16),
        pltpu.VMEM((ROWS, C), f32),
        pltpu.VMEM((ROWS, D), f32),
        pltpu.VMEM((HALF, D), bf16),
        pltpu.VMEM((ROWS, C), i32),
        pltpu.VMEM((8, HALF), i32),
        pltpu.VMEM((8, C), f32),
    )
    held = pl.pallas_call(
        exchange_kernel,
        out_shape=handed_on,
        in_specs=[hbm] * 4 + [smem] * 2,
        out_specs=(vmem,) * len(handed_on),
        scratch_shapes=[
            pltpu.VMEM((ROWS, D), bf16),
            pltpu.VMEM((ROWS, D), bf16),
            pltpu.VMEM((ROWS, C), f32),
            pltpu.VMEM((ROWS, D), f32),
            pltpu.VMEM((2, ROWS, D), bf16),
            pltpu.VMEM((2, ROWS), i32),
            pltpu.VMEM((2, ROWS), i32),
            pltpu.VMEM((ROWS, C), i32),
            pltpu.VMEM((2, FULL + 1, 8, C), i32),
            pltpu.VMEM((ROWS, C), f32),
            dma((2,)), dma((2,)), dma((2, FULL + 2)), dma((2, FULL + 2)), dma((2,)), dma((2,)),
            pltpu.SemaphoreType.REGULAR((2,)),
        ],
        compiler_params=pltpu.CompilerParams(
            collective_id=0, has_side_effects=True, vmem_limit_bytes=28 << 20
        ),
        name="exchange_and_grads",
    )(*operands, log_scale, logit_bias)
    held = [pltpu.with_memory_space_constraint(x, pltpu.VMEM) for x in held]
    return pl.pallas_call(
        finish_kernel,
        out_shape=(pltpu.HBM((ROWS,), f32), pltpu.HBM((ROWS, D), bf16), pltpu.HBM((ROWS, D), bf16)),
        in_specs=[vmem] * len(handed_on),
        out_specs=(hbm,) * 3,
        scratch_shapes=[pltpu.VMEM((ROWS, D), bf16), dma((2 + ROWS // BLOCK,))],
        compiler_params=pltpu.CompilerParams(vmem_limit_bytes=12 << 20),
        name="finish_text_side",
    )(*held)


def solution(mesh):
    blocks = P(("img", "txt"))
    rows = P(("img", "txt"), None)
    return jax.shard_map(
        body,
        mesh=mesh,
        in_specs=(rows, rows, blocks, blocks, P(), P()),
        out_specs=(blocks, rows, rows),
        check_vma=False,
    )
```

```python
import jax
import jax.numpy as jnp
from jax import lax
from jax.experimental import pallas as pl
from jax.experimental.pallas import tpu as pltpu
from jax.sharding import PartitionSpec as P

MESH = pl.DeviceIdType.MESH
ROWS, D = 512, 1152
C = 128
FULL = ROWS // C - 1
HALF = C // 2
BLOCK = 128
TEXT, IMAGE = 0, 1


def inverse_norm(x):
    return lax.rsqrt(jnp.sum(x * x, axis=1, keepdims=True) + 1e-06)


def unit_rows(rows):
    x = rows.astype(jnp.float32)
    return (x * inverse_norm(x)).astype(jnp.bfloat16)


def slopes_of(own_unit, other_unit, same, scale, bias):
    dots = lax.dot_general(
        own_unit, other_unit, (((1,), (1,)), ((), ())), preferred_element_type=jnp.float32
    )
    logits = dots * scale + bias
    margins = jnp.where(same, logits, -logits)
    e = jnp.exp(-jnp.abs(margins))
    recip = 1.0 / (1.0 + e)
    sigmoid = jnp.where(margins >= 0, e * recip, recip)
    slopes = (jnp.where(same, -scale, scale) * sigmoid).astype(jnp.bfloat16)
    return slopes, dots, lambda: jnp.maximum(-margins, 0.0) + jnp.log1p(e)


def back_norm(rows, r, g):
    x = rows.astype(jnp.float32)
    inner = jnp.sum(x * g, axis=1, keepdims=True)
    return r * g - (r * r * r * inner) * x


def exchange_kernel(
    img, txt, img_ids, txt_ids, log_scale, logit_bias,
    loss, image_grad, text_own, text_unit, text_inv, text_base, last_unit, text_id_col, last_id_row, constants,
    image_own, image_unit, image_inv, image_acc, got, own_ids, got_ids, image_id_col, id_row, loss_acc,
    own_sem, own_id_sem, send_sem, recv_sem, id_send_sem, id_recv_sem, ack_sem,
):
    n_img, n_txt = lax.axis_size("img"), lax.axis_size("txt")
    p, q = lax.axis_index("img"), lax.axis_index("txt")
    text_to = (lax.rem(p + 1, n_img), lax.rem(q + n_txt - 1, n_txt))
    image_to = (lax.rem(p + n_img - 1, n_img), lax.rem(q + 1, n_txt))

    n_z = n_txt // 2
    z, core, y_hi = lax.rem(q, n_z), lax.rem(p, 2), lax.rem(p // 2, 2)
    near_to = (jnp.where(core == 0, text_to[0], image_to[0]), jnp.where(core == 0, text_to[1], image_to[1]))
    far_to = (jnp.where(core == 0, image_to[0], text_to[0]), jnp.where(core == 0, image_to[1], text_to[1]))
    first, last = jnp.int32(z == 0), jnp.int32(z == n_z - 1)
    both = jnp.where(core == 0, y_hi, 1 - y_hi)
    from_last = jnp.maximum(first, last)
    to_last = jnp.maximum(jnp.int32(z == n_z - 2), last)
    near_signals = jnp.where(core == 0, from_last, 1 - to_last)
    near_direct = 1 - near_signals
    near_acks = near_direct
    far_signals = jnp.where(core == 0, 1 - to_last, jnp.maximum(from_last, both))
    far_direct = jnp.where(core == 0, jnp.maximum(to_last, both), 1 - from_last)
    far_acks = jnp.where(core == 0, to_last, (1 - from_last) * (1 - both))
    image_direct = jnp.where(core == 0, far_direct, near_direct)
    text_direct = jnp.where(core == 0, near_direct, far_direct)

    barrier = pltpu.get_barrier_semaphore()
    for signals, partner in ((near_signals, near_to), (far_signals, far_to)):

        @pl.when(signals == 1)
        def _():
            pl.semaphore_signal(barrier, inc=1, device_id=partner, device_id_type=MESH)

    sources, source_ids, targets = (txt, img), (txt_ids, img_ids), (text_to, image_to)
    own, unit, inv, acc = (
        (image_own, text_own), (image_unit, text_unit), (image_inv, text_inv), (image_acc, text_base),
    )
    id_col = (image_id_col, text_id_col)
    pieces = (
        [(k * C, C) for k in range(FULL + 1)],
        [(k * C, C) for k in range(FULL)] + [(FULL * C, HALF)],
    )

    def id_copy(side):
        return pltpu.make_async_remote_copy(
            src_ref=source_ids[side], dst_ref=got_ids.at[side],
            send_sem=id_send_sem.at[side], recv_sem=id_recv_sem.at[side],
            device_id=targets[side], device_id_type=MESH,
        )

    def piece_copy(side, k, start, size, source=None):
        rows = pl.ds(start, size)
        return pltpu.make_async_remote_copy(
            src_ref=(sources[side] if source is None else source).at[rows], dst_ref=got.at[side, rows],
            send_sem=send_sem.at[side, k], recv_sem=recv_sem.at[side, k],
            device_id=targets[side], device_id_type=MESH,
        )

    def sends(side):
        rows = [piece_copy(side, k, *piece) for k, piece in enumerate(pieces[side])]
        return rows[:1] + [id_copy(side)] + rows[1:]

    def last_send():
        return piece_copy(IMAGE, FULL + 1, FULL * C + HALF, HALF, image_unit)

    loads = []
    for side, ref, ids in ((TEXT, img, img_ids), (IMAGE, txt, txt_ids)):
        loads.append(pltpu.make_async_copy(ids, own_ids.at[side], own_id_sem.at[side]))
        loads.append(pltpu.make_async_copy(ref, own[side], own_sem.at[side]))
    def start_sends(side):
        for copy in sends(side):
            copy.start()

    n_direct = near_direct + far_direct

    @pl.when(n_direct > 0)
    def _():
        pl.semaphore_wait(barrier, n_direct)

    pl.when(image_direct == 1)(lambda: start_sends(IMAGE))
    for i, (acks, partner) in enumerate(((near_acks, near_to), (far_acks, far_to))):

        @pl.when(acks == 1)
        def _():
            pl.semaphore_signal(ack_sem.at[i], inc=1, device_id=partner, device_id_type=MESH)

    image_ack = jnp.where(core == 0, 1, 0)
    pl.when(text_direct == 1)(lambda: start_sends(TEXT))
    for copy in loads:
        copy.start()
    def send_when_acknowledged(side, ack):
        pl.semaphore_wait(ack_sem.at[ack], 1)
        start_sends(side)

    @pl.when(image_direct == 0)
    def _():
        send_when_acknowledged(IMAGE, image_ack)

    @pl.when((1 - text_direct) * (1 - last) == 1)
    def _():
        send_when_acknowledged(TEXT, 1 - image_ack)

    scale = jnp.exp(jnp.full((1, C), log_scale[0], jnp.float32))
    bias = jnp.full((1, C), logit_bias[0], jnp.float32)
    constants[0:1, :] = scale
    constants[1:2, :] = bias

    for copy in loads:
        copy.wait()

    for side in (TEXT, IMAGE):
        for k in range(FULL + 1):
            piece = pl.ds(k * C, C)
            row = own_ids[side, piece].reshape(1, C)
            id_row[1 - side, k] = jnp.broadcast_to(row, (8, C))
            id_col[side][piece, :] = jnp.broadcast_to(row, (C, C)).T

        @pl.loop(0, FULL + 1)
        def _(k):
            piece = pl.ds(k * C, C)
            x = own[side][piece, :].astype(jnp.float32)
            r = inverse_norm(x)
            inv[side][piece, :] = jnp.broadcast_to(r, (C, C))
            unit[side][piece, :] = (x * r).astype(jnp.bfloat16)

        if side == TEXT:
            last_send().start()

            @pl.when((1 - text_direct) * last == 1)
            def _():
                send_when_acknowledged(TEXT, 1 - image_ack)

    loss_acc[...] = jnp.zeros_like(loss_acc)
    for side in (TEXT, IMAGE):
        acc[side][...] = jnp.zeros_like(acc[side])

    def slopes_on(side, other_unit, other_ids):
        width = other_unit.shape[0]
        same = id_col[side][:, :width] == other_ids
        slopes, _, loss_terms = slopes_of(unit[side][...], other_unit, same, scale[:, :width], bias[:, :width])
        if side == TEXT:
            loss_acc[...] += loss_terms()
        return slopes

    def add_chunk(side, other_unit, other_ids):
        slopes = slopes_on(side, other_unit, other_ids)
        acc[side][...] += jnp.dot(slopes, other_unit, preferred_element_type=jnp.float32)

    for side in (TEXT, IMAGE):

        @pl.loop(0, FULL + 1)
        def _(k):
            add_chunk(side, unit[1 - side][pl.ds(k * C, C), :], id_row[side, k][0:1])

    for side in (TEXT, IMAGE):
        id_copy(side).wait_recv()
        for k in range(FULL + 1):
            row = got_ids[side, pl.ds(k * C, C)].reshape(1, C)
            id_row[side, k] = jnp.broadcast_to(row, (8, C))

    def arrived(side, k, start, size):
        piece_copy(side, k, start, size).wait_recv()
        return unit_rows(got[side, pl.ds(start, size), :])

    @pl.loop(0, FULL)
    def _(k):
        for side in (TEXT, IMAGE):
            other = arrived(side, k, k * C, C)
            add_chunk(side, other, id_row[side, k][0:1])

    def finish_text():
        other = arrived(TEXT, FULL, FULL * C, C)
        slopes = slopes_on(TEXT, other, id_row[TEXT, FULL][0:1])
        for b in range(ROWS // BLOCK):
            rows = pl.ds(b * BLOCK, BLOCK)
            g = image_acc[rows, :] + jnp.dot(
                slopes[b * BLOCK : (b + 1) * BLOCK], other, preferred_element_type=jnp.float32
            )
            grad = back_norm(image_own[rows, :], image_inv[rows, 0:1], g)
            image_grad[rows, :] = grad.astype(jnp.bfloat16)
        loss[...] = jnp.sum(loss_acc[...].T, axis=0, keepdims=True).reshape(ROWS)

    pl.when(first == 1)(finish_text)

    other = arrived(IMAGE, FULL, FULL * C, HALF)
    last_ids = id_row[IMAGE, FULL]
    add_chunk(IMAGE, other, last_ids[0:1, :HALF])
    last_id_row[...] = jnp.broadcast_to(last_ids[0:1, HALF:], (8, HALF))
    for b in range(ROWS // BLOCK):
        rows = pl.ds(b * BLOCK, BLOCK)
        text_base[rows, :] = back_norm(text_own[rows, :], text_inv[rows, 0:1], text_base[rows, :])

    pl.when(first == 0)(finish_text)

    for copy in sends(TEXT) + sends(IMAGE) + [last_send()]:
        copy.wait_send()
    last_send().wait_recv()
    last_unit[...] = got[IMAGE, pl.ds(FULL * C + HALF, HALF), :]


def finish_kernel(
    loss, image_grad, own, unit, inv, base, last_unit, id_col, last_id_row, constants,
    loss_out, image_out, text_out,
    stage, sem,
):
    copies = [
        pltpu.make_async_copy(loss, loss_out, sem.at[0]),
        pltpu.make_async_copy(image_grad, image_out, sem.at[1]),
    ]
    for copy in copies:
        copy.start()
    other = last_unit[...]
    scale, bias = constants[0:1, :HALF], constants[1:2, :HALF]

    def slopes_and_inner(b):
        rows = pl.ds(b * BLOCK, BLOCK)
        same = id_col[rows, :HALF] == last_id_row[0:1]
        slopes, dots, _ = slopes_of(unit[rows, :], other, same, scale, bias)
        return slopes, jnp.sum(slopes.astype(jnp.float32) * dots, axis=1, keepdims=True)

    blocks = ROWS // BLOCK
    ahead = slopes_and_inner(0)
    for b in range(blocks):
        slopes, inner = ahead
        if b + 1 < blocks:
            ahead = slopes_and_inner(b + 1)
        rows = pl.ds(b * BLOCK, BLOCK)
        r = inv[rows, 0:1]
        h = jnp.dot(slopes, other, preferred_element_type=jnp.float32)
        grad = base[rows, :] + r * h - (r * r * inner) * own[rows, :].astype(jnp.float32)
        stage[rows, :] = grad.astype(jnp.bfloat16)
        copy = pltpu.make_async_copy(stage.at[rows], text_out.at[rows], sem.at[2 + b])
        copy.start()
        copies.append(copy)
    for copy in copies:
        copy.wait()


def body(image_rows, text_rows, image_ids, text_ids, log_scale, logit_bias):
    bf16, f32, i32 = jnp.bfloat16, jnp.float32, jnp.int32
    hbm = pl.BlockSpec(memory_space=pltpu.HBM)
    vmem = pl.BlockSpec(memory_space=pltpu.VMEM)
    smem = pl.BlockSpec(memory_space=pltpu.SMEM)
    dma = pltpu.SemaphoreType.DMA
    operands = [
        pltpu.with_memory_space_constraint(x, pltpu.HBM)
        for x in (image_rows, text_rows, image_ids, text_ids)
    ]
    handed_on = (
        pltpu.VMEM((ROWS,), f32),
        pltpu.VMEM((ROWS, D), bf16),
        pltpu.VMEM((ROWS, D), bf16),
        pltpu.VMEM((ROWS, D), bf16),
        pltpu.VMEM((ROWS, C), f32),
        pltpu.VMEM((ROWS, D), f32),
        pltpu.VMEM((HALF, D), bf16),
        pltpu.VMEM((ROWS, C), i32),
        pltpu.VMEM((8, HALF), i32),
        pltpu.VMEM((8, C), f32),
    )
    held = pl.pallas_call(
        exchange_kernel,
        out_shape=handed_on,
        in_specs=[hbm] * 4 + [smem] * 2,
        out_specs=(vmem,) * len(handed_on),
        scratch_shapes=[
            pltpu.VMEM((ROWS, D), bf16),
            pltpu.VMEM((ROWS, D), bf16),
            pltpu.VMEM((ROWS, C), f32),
            pltpu.VMEM((ROWS, D), f32),
            pltpu.VMEM((2, ROWS, D), bf16),
            pltpu.VMEM((2, ROWS), i32),
            pltpu.VMEM((2, ROWS), i32),
            pltpu.VMEM((ROWS, C), i32),
            pltpu.VMEM((2, FULL + 1, 8, C), i32),
            pltpu.VMEM((ROWS, C), f32),
            dma((2,)), dma((2,)), dma((2, FULL + 2)), dma((2, FULL + 2)), dma((2,)), dma((2,)),
            pltpu.SemaphoreType.REGULAR((2,)),
        ],
        compiler_params=pltpu.CompilerParams(
            collective_id=0, has_side_effects=True, vmem_limit_bytes=28 << 20
        ),
        name="exchange_and_grads",
    )(*operands, log_scale, logit_bias)
    held = [pltpu.with_memory_space_constraint(x, pltpu.VMEM) for x in held]
    return pl.pallas_call(
        finish_kernel,
        out_shape=(pltpu.HBM((ROWS,), f32), pltpu.HBM((ROWS, D), bf16), pltpu.HBM((ROWS, D), bf16)),
        in_specs=[vmem] * len(handed_on),
        out_specs=(hbm,) * 3,
        scratch_shapes=[pltpu.VMEM((ROWS, D), bf16), dma((2 + ROWS // BLOCK,))],
        compiler_params=pltpu.CompilerParams(vmem_limit_bytes=12 << 20),
        name="finish_text_side",
    )(*held)


def solution(mesh):
    blocks = P(("img", "txt"))
    rows = P(("img", "txt"), None)
    return jax.shard_map(
        body,
        mesh=mesh,
        in_specs=(rows, rows, blocks, blocks, P(), P()),
        out_specs=(blocks, rows, rows),
        check_vma=False,
    )
```

```python
import jax
import jax.numpy as jnp
from jax import lax
from jax.experimental import pallas as pl
from jax.experimental.pallas import tpu as pltpu
from jax.sharding import PartitionSpec as P

MESH = pl.DeviceIdType.MESH
ROWS, D = 512, 1152
C = 128
FULL = ROWS // C - 1
HALF = C // 2
BLOCK = 128
TEXT, IMAGE = 0, 1


def inverse_norm(x):
    return lax.rsqrt(jnp.sum(x * x, axis=1, keepdims=True) + 1e-06)


def unit_rows(rows):
    x = rows.astype(jnp.float32)
    return (x * inverse_norm(x)).astype(jnp.bfloat16)


def slopes_of(own_unit, other_unit, same, scale, bias):
    dots = lax.dot_general(
        own_unit, other_unit, (((1,), (1,)), ((), ())), preferred_element_type=jnp.float32
    )
    logits = dots * scale + bias
    margins = jnp.where(same, logits, -logits)
    e = jnp.exp(-jnp.abs(margins))
    recip = 1.0 / (1.0 + e)
    sigmoid = jnp.where(margins >= 0, e * recip, recip)
    slopes = (jnp.where(same, -scale, scale) * sigmoid).astype(jnp.bfloat16)
    return slopes, dots, lambda: jnp.maximum(-margins, 0.0) + jnp.log1p(e)


def back_norm(rows, r, g):
    x = rows.astype(jnp.float32)
    inner = jnp.sum(x * g, axis=1, keepdims=True)
    return r * g - (r * r * r * inner) * x


def exchange_kernel(
    img, txt, img_ids, txt_ids, log_scale, logit_bias,
    loss, image_grad, text_own, text_unit, text_inv, text_coef, text_base, last_unit, text_id_col, last_id_row, constants,
    image_own, image_unit, image_inv, image_acc, got, own_ids, got_ids, image_id_col, id_row, loss_acc,
    own_sem, own_id_sem, send_sem, recv_sem, id_send_sem, id_recv_sem, ack_sem,
):
    n_img, n_txt = lax.axis_size("img"), lax.axis_size("txt")
    p, q = lax.axis_index("img"), lax.axis_index("txt")
    text_to = (lax.rem(p + 1, n_img), lax.rem(q + n_txt - 1, n_txt))
    image_to = (lax.rem(p + n_img - 1, n_img), lax.rem(q + 1, n_txt))

    n_z = n_txt // 2
    z, core, y_hi = lax.rem(q, n_z), lax.rem(p, 2), lax.rem(p // 2, 2)
    near_to = (jnp.where(core == 0, text_to[0], image_to[0]), jnp.where(core == 0, text_to[1], image_to[1]))
    far_to = (jnp.where(core == 0, image_to[0], text_to[0]), jnp.where(core == 0, image_to[1], text_to[1]))
    first, last = jnp.int32(z == 0), jnp.int32(z == n_z - 1)
    both = jnp.where(core == 0, y_hi, 1 - y_hi)
    from_last = jnp.maximum(first, last)
    to_last = jnp.maximum(jnp.int32(z == n_z - 2), last)
    near_signals = jnp.where(core == 0, from_last, 1 - to_last)
    near_direct = 1 - near_signals
    near_acks = near_direct
    far_signals = jnp.where(core == 0, 1 - to_last, jnp.maximum(from_last, both))
    far_direct = jnp.where(core == 0, jnp.maximum(to_last, both), 1 - from_last)
    far_acks = jnp.where(core == 0, to_last, (1 - from_last) * (1 - both))
    image_direct = jnp.where(core == 0, far_direct, near_direct)
    text_direct = jnp.where(core == 0, near_direct, far_direct)

    barrier = pltpu.get_barrier_semaphore()
    for signals, partner in ((near_signals, near_to), (far_signals, far_to)):

        @pl.when(signals == 1)
        def _():
            pl.semaphore_signal(barrier, inc=1, device_id=partner, device_id_type=MESH)

    sources, source_ids, targets = (txt, img), (txt_ids, img_ids), (text_to, image_to)
    own, unit, inv, acc = (
        (image_own, text_own), (image_unit, text_unit), (image_inv, text_inv), (image_acc, text_base),
    )
    id_col = (image_id_col, text_id_col)
    pieces = (
        [(k * C, C) for k in range(FULL + 1)],
        [(k * C, C) for k in range(FULL)] + [(FULL * C, HALF), (FULL * C + HALF, HALF)],
    )

    def id_copy(side):
        return pltpu.make_async_remote_copy(
            src_ref=source_ids[side], dst_ref=got_ids.at[side],
            send_sem=id_send_sem.at[side], recv_sem=id_recv_sem.at[side],
            device_id=targets[side], device_id_type=MESH,
        )

    def piece_copy(side, k, start, size):
        rows = pl.ds(start, size)
        return pltpu.make_async_remote_copy(
            src_ref=sources[side].at[rows], dst_ref=got.at[side, rows],
            send_sem=send_sem.at[side, k], recv_sem=recv_sem.at[side, k],
            device_id=targets[side], device_id_type=MESH,
        )

    def sends(side):
        return [id_copy(side)] + [piece_copy(side, k, *piece) for k, piece in enumerate(pieces[side])]

    loads = []
    for side, ref, ids in ((TEXT, img, img_ids), (IMAGE, txt, txt_ids)):
        loads.append(pltpu.make_async_copy(ids, own_ids.at[side], own_id_sem.at[side]))
        loads.append(pltpu.make_async_copy(ref, own[side], own_sem.at[side]))
    for copy in loads:
        copy.start()

    def start_sends(side):
        for copy in sends(side):
            copy.start()

    n_direct = near_direct + far_direct

    @pl.when(n_direct > 0)
    def _():
        pl.semaphore_wait(barrier, n_direct)

    for i, (acks, partner) in enumerate(((near_acks, near_to), (far_acks, far_to))):

        @pl.when(acks == 1)
        def _():
            pl.semaphore_signal(ack_sem.at[i], inc=1, device_id=partner, device_id_type=MESH)

    image_ack = jnp.where(core == 0, 1, 0)
    pl.when(image_direct == 1)(lambda: start_sends(IMAGE))
    pl.when(text_direct == 1)(lambda: start_sends(TEXT))
    for side, direct, ack in ((IMAGE, image_direct, image_ack), (TEXT, text_direct, 1 - image_ack)):

        @pl.when(direct == 0)
        def _():
            pl.semaphore_wait(ack_sem.at[ack], 1)
            start_sends(side)

    scale = jnp.exp(jnp.full((1, C), log_scale[0], jnp.float32))
    bias = jnp.full((1, C), logit_bias[0], jnp.float32)
    constants[0:1, :] = scale
    constants[1:2, :] = bias

    for copy in loads:
        copy.wait()

    for side in (TEXT, IMAGE):
        for k in range(FULL + 1):
            piece = pl.ds(k * C, C)
            row = own_ids[side, piece].reshape(1, C)
            id_row[1 - side, k] = jnp.broadcast_to(row, (8, C))
            id_col[side][piece, :] = jnp.broadcast_to(row, (C, C)).T

        @pl.loop(0, FULL + 1)
        def _(k):
            piece = pl.ds(k * C, C)
            x = own[side][piece, :].astype(jnp.float32)
            r = inverse_norm(x)
            inv[side][piece, :] = jnp.broadcast_to(r, (C, C))
            rounded = (x * r).astype(jnp.bfloat16)
            unit[side][piece, :] = rounded
            if side == IMAGE:
                u = rounded.astype(jnp.float32)
                squares = jnp.maximum(jnp.sum(u * u, axis=1, keepdims=True), 1e-30)
                ratio = jnp.sum(x * u, axis=1, keepdims=True) / squares
                text_coef[piece, :] = jnp.broadcast_to(r * r * r * ratio, (C, C))

    loss_acc[...] = jnp.zeros_like(loss_acc)
    for side in (TEXT, IMAGE):
        acc[side][...] = jnp.zeros_like(acc[side])

    def slopes_on(side, other_unit, other_ids):
        width = other_unit.shape[0]
        same = id_col[side][:, :width] == other_ids
        slopes, _, loss_terms = slopes_of(unit[side][...], other_unit, same, scale[:, :width], bias[:, :width])
        if side == TEXT:
            loss_acc[...] += loss_terms()
        return slopes

    def add_chunk(side, other_unit, other_ids):
        slopes = slopes_on(side, other_unit, other_ids)
        acc[side][...] += jnp.dot(slopes, other_unit, preferred_element_type=jnp.float32)

    for side in (TEXT, IMAGE):

        @pl.loop(0, FULL + 1)
        def _(k):
            add_chunk(side, unit[1 - side][pl.ds(k * C, C), :], id_row[side, k][0:1])

    for side in (TEXT, IMAGE):
        id_copy(side).wait_recv()
        for k in range(FULL + 1):
            row = got_ids[side, pl.ds(k * C, C)].reshape(1, C)
            id_row[side, k] = jnp.broadcast_to(row, (8, C))

    def arrived(side, k, start, size):
        piece_copy(side, k, start, size).wait_recv()
        return unit_rows(got[side, pl.ds(start, size), :])

    @pl.loop(0, FULL)
    def _(k):
        for side in (TEXT, IMAGE):
            other = arrived(side, k, k * C, C)
            add_chunk(side, other, id_row[side, k][0:1])

    def finish_text():
        other = arrived(TEXT, FULL, FULL * C, C)
        slopes = slopes_on(TEXT, other, id_row[TEXT, FULL][0:1])
        for b in range(ROWS // BLOCK):
            rows = pl.ds(b * BLOCK, BLOCK)
            g = image_acc[rows, :] + jnp.dot(
                slopes[b * BLOCK : (b + 1) * BLOCK], other, preferred_element_type=jnp.float32
            )
            grad = back_norm(image_own[rows, :], image_inv[rows, 0:1], g)
            image_grad[rows, :] = grad.astype(jnp.bfloat16)
        loss[...] = jnp.sum(loss_acc[...].T, axis=0, keepdims=True).reshape(ROWS)

    pl.when(first == 1)(finish_text)

    other = arrived(IMAGE, FULL, FULL * C, HALF)
    last_ids = id_row[IMAGE, FULL]
    add_chunk(IMAGE, other, last_ids[0:1, :HALF])
    last_id_row[...] = jnp.broadcast_to(last_ids[0:1, HALF:], (8, HALF))
    for b in range(ROWS // BLOCK):
        rows = pl.ds(b * BLOCK, BLOCK)
        text_base[rows, :] = back_norm(text_own[rows, :], text_inv[rows, 0:1], text_base[rows, :])

    pl.when(first == 0)(finish_text)

    for side in (TEXT, IMAGE):
        for copy in sends(side):
            copy.wait_send()
    last_unit[...] = arrived(IMAGE, FULL + 1, FULL * C + HALF, HALF)


def finish_kernel(
    loss, image_grad, own, unit, inv, coef, base, last_unit, id_col, last_id_row, constants,
    loss_out, image_out, text_out,
    stage, sem,
):
    copies = [
        pltpu.make_async_copy(loss, loss_out, sem.at[0]),
        pltpu.make_async_copy(image_grad, image_out, sem.at[1]),
    ]
    for copy in copies:
        copy.start()
    other = last_unit[...]
    scale, bias = constants[0:1, :HALF], constants[1:2, :HALF]

    def slopes_and_inner(b):
        rows = pl.ds(b * BLOCK, BLOCK)
        same = id_col[rows, :HALF] == last_id_row[0:1]
        slopes, dots, _ = slopes_of(unit[rows, :], other, same, scale, bias)
        return slopes, jnp.sum(slopes.astype(jnp.float32) * dots, axis=1, keepdims=True)

    blocks = ROWS // BLOCK
    ahead = slopes_and_inner(0)
    for b in range(blocks):
        slopes, inner = ahead
        if b + 1 < blocks:
            ahead = slopes_and_inner(b + 1)
        rows = pl.ds(b * BLOCK, BLOCK)
        r = inv[rows, 0:1]
        h = jnp.dot(slopes, other, preferred_element_type=jnp.float32)
        grad = base[rows, :] + r * h - (coef[rows, 0:1] * inner) * own[rows, :].astype(jnp.float32)
        stage[rows, :] = grad.astype(jnp.bfloat16)
        copy = pltpu.make_async_copy(stage.at[rows], text_out.at[rows], sem.at[2 + b])
        copy.start()
        copies.append(copy)
    for copy in copies:
        copy.wait()


def body(image_rows, text_rows, image_ids, text_ids, log_scale, logit_bias):
    bf16, f32, i32 = jnp.bfloat16, jnp.float32, jnp.int32
    hbm = pl.BlockSpec(memory_space=pltpu.HBM)
    vmem = pl.BlockSpec(memory_space=pltpu.VMEM)
    smem = pl.BlockSpec(memory_space=pltpu.SMEM)
    dma = pltpu.SemaphoreType.DMA
    operands = [
        pltpu.with_memory_space_constraint(x, pltpu.HBM)
        for x in (image_rows, text_rows, image_ids, text_ids)
    ]
    handed_on = (
        pltpu.VMEM((ROWS,), f32),
        pltpu.VMEM((ROWS, D), bf16),
        pltpu.VMEM((ROWS, D), bf16),
        pltpu.VMEM((ROWS, D), bf16),
        pltpu.VMEM((ROWS, C), f32),
        pltpu.VMEM((ROWS, C), f32),
        pltpu.VMEM((ROWS, D), f32),
        pltpu.VMEM((HALF, D), bf16),
        pltpu.VMEM((ROWS, C), i32),
        pltpu.VMEM((8, HALF), i32),
        pltpu.VMEM((8, C), f32),
    )
    held = pl.pallas_call(
        exchange_kernel,
        out_shape=handed_on,
        in_specs=[hbm] * 4 + [smem] * 2,
        out_specs=(vmem,) * len(handed_on),
        scratch_shapes=[
            pltpu.VMEM((ROWS, D), bf16),
            pltpu.VMEM((ROWS, D), bf16),
            pltpu.VMEM((ROWS, C), f32),
            pltpu.VMEM((ROWS, D), f32),
            pltpu.VMEM((2, ROWS, D), bf16),
            pltpu.VMEM((2, ROWS), i32),
            pltpu.VMEM((2, ROWS), i32),
            pltpu.VMEM((ROWS, C), i32),
            pltpu.VMEM((2, FULL + 1, 8, C), i32),
            pltpu.VMEM((ROWS, C), f32),
            dma((2,)), dma((2,)), dma((2, FULL + 2)), dma((2, FULL + 2)), dma((2,)), dma((2,)),
            pltpu.SemaphoreType.REGULAR((2,)),
        ],
        compiler_params=pltpu.CompilerParams(
            collective_id=0, has_side_effects=True, vmem_limit_bytes=28 << 20
        ),
        name="exchange_and_grads",
    )(*operands, log_scale, logit_bias)
    held = [pltpu.with_memory_space_constraint(x, pltpu.VMEM) for x in held]
    return pl.pallas_call(
        finish_kernel,
        out_shape=(pltpu.HBM((ROWS,), f32), pltpu.HBM((ROWS, D), bf16), pltpu.HBM((ROWS, D), bf16)),
        in_specs=[vmem] * len(handed_on),
        out_specs=(hbm,) * 3,
        scratch_shapes=[pltpu.VMEM((ROWS, D), bf16), dma((2 + ROWS // BLOCK,))],
        compiler_params=pltpu.CompilerParams(vmem_limit_bytes=12 << 20),
        name="finish_text_side",
    )(*held)


def solution(mesh):
    blocks = P(("img", "txt"))
    rows = P(("img", "txt"), None)
    return jax.shard_map(
        body,
        mesh=mesh,
        in_specs=(rows, rows, blocks, blocks, P(), P()),
        out_specs=(blocks, rows, rows),
        check_vma=False,
    )
```
